32 devices in a mesh: fsdp: 8 (over y, x, core), rep: 4 (over z).
Axes of the slice: x: 2, y: 2, z: 4, core: 2. Of those that a mesh axis runs over, the one named last changes fastest.
Arguments:
- student_hidden: bfloat16 [6144, 3072], P(('fsdp', 'rep')), may hold values from -6 to 6
- out_cotangent: bfloat16 [6144, 768], P(('fsdp', 'rep')), may hold values from -0.078125 to 0.078125
- student_branch: bfloat16 [6144, 768], P(('fsdp', 'rep')), may hold values from -6 to 6
- layer_scale: float32 [768], replicated, may hold values from 0.1 to 1
- scale_first: float32 [768], replicated, may hold values from -1.75 to 1.75
- scale_second: float32 [768], replicated, may hold values from 0.05 to 1
- student_weight: bfloat16 [3072, 768], P(('fsdp', 'rep')), may hold values from -0.109375 to 0.109375
- first_moment: bfloat16 [3072, 768], P(('fsdp', 'rep')), may hold values from -0.1875 to 0.1875
- second_moment: bfloat16 [3072, 768], P(('fsdp', 'rep')), may hold values from 0.0019989014 to 0.049804688
- teacher_weight: bfloat16 [3072, 768], P('fsdp'), may hold values from -0.109375 to 0.109375
- teacher_scale: float32 [768], replicated, may hold values from 0.1 to 1
- teacher_hidden: bfloat16 [8192, 3072], P(('fsdp', 'rep')), may hold values from -6 to 6
- teacher_input: bfloat16 [8192, 768], P(('fsdp', 'rep')), may hold values from -6 to 6
Outputs:
- new_weight: bfloat16 [3072, 768], P(('fsdp', 'rep'))
- new_first: bfloat16 [3072, 768], P(('fsdp', 'rep'))
- new_second: bfloat16 [3072, 768], P(('fsdp', 'rep'))
- new_teacher: bfloat16 [3072, 768], P('fsdp')
- new_scale: float32 [768], replicated
- new_scale_first: float32 [768], replicated
- new_scale_second: float32 [768], replicated
- new_teacher_scale: float32 [768], replicated
- teacher_out: bfloat16 [8192, 768], P(('fsdp', 'rep'))
The draws below stay inside these ranges and needn't reach their ends.
All inputs are finite; a program needn't handle non-finite values.
Results may differ from the reference program's by a relative error of at most 0.0048.
Values may be sent and summed in bfloat16 or wider, within the bound.
No kernel may reach another device: no remote copies, remote signals or barrier semaphores. Data moves between devices by JAX's collectives and lax.ppermute only.
A program may use at most 64 MiB of HBM per device.

```python
import math
import jax
import jax.numpy as jnp
from jax import lax

D = 768
FF = 3072
STUDENT_TOKENS = 6144
TEACHER_TOKENS = 8192


def block_scale(stream_key, dims, shards, least, largest):
    def one(position, blocks):
        draws = jax.random.uniform(jax.random.fold_in(jax.random.fold_in(stream_key, 6), position), (blocks,), jnp.float32, least / len(shards), largest / len(shards))
        return jnp.repeat(jnp.exp(draws), dims[position] // blocks).reshape((-1,) + (1,) * (len(dims) - position - 1))

    factor_of = one(*shards[0])
    for cut in shards[1:]:
        factor_of = factor_of * one(*cut)
    return factor_of


def normal_values(stream_key, dims, scale, reach, shards=(), held_as=jnp.bfloat16):
    result = scale * jax.random.normal(stream_key, dims, jnp.float32)
    if shards:
        result = result * block_scale(stream_key, dims, shards, -0.22, 0.18)
    return jnp.clip(result, -reach, reach).astype(held_as)


def setup_inputs(seed: int = 0) -> dict:
    splits = jax.random.split(jax.random.key(seed), 14)
    return {
        "student_hidden": normal_values(splits[0], (STUDENT_TOKENS, FF), 1.0, 6.0, ((0, 32),)),
        "out_cotangent": normal_values(splits[1], (STUDENT_TOKENS, D), (1.0 / STUDENT_TOKENS ** 0.5), 0.078125, ((0, 32),)),
        "student_branch": normal_values(splits[2], (STUDENT_TOKENS, D), 1.0, 6.0, ((0, 32),)),
        "layer_scale": jnp.clip(jnp.exp(jax.random.uniform(splits[3], (D,), jnp.float32, math.log(0.1), math.log(1.0))), 0.1, 1.0),
        "scale_first": normal_values(splits[4], (D,), 0.3, 1.75, (), jnp.float32),
        "scale_second": jnp.clip(jnp.exp(jax.random.uniform(splits[5], (D,), jnp.float32, math.log(0.05), math.log(1.0))), 0.05, 1.0),
        "student_weight": normal_values(splits[6], (FF, D), FF ** -0.5, 0.109375, ((0, 32),)),
        "first_moment": normal_values(splits[7], (FF, D), 0.03, 0.1875, ((0, 32),)),
        "second_moment": jnp.clip(jnp.exp(math.log(0.049804688) - 3.2155114 * jax.random.uniform(splits[8], (FF, D), jnp.float32) ** block_scale(splits[8], (FF, D), ((0, 32),), -0.2, 0.2)), 0.0019989014, 0.049804688).astype(jnp.bfloat16),
        "teacher_weight": normal_values(splits[9], (FF, D), FF ** -0.5, 0.109375, ((0, 8),)),
        "teacher_scale": jnp.clip(jnp.exp(jax.random.uniform(splits[10], (D,), jnp.float32, math.log(0.1), math.log(1.0))), 0.1, 1.0),
        "teacher_hidden": normal_values(splits[11], (TEACHER_TOKENS, FF), 1.0, 6.0, ((0, 32),)),
        "teacher_input": normal_values(splits[12], (TEACHER_TOKENS, D), 1.0, 6.0, ((0, 32),)),
    }


beta_one = 0.9
beta_two = 0.95
learn_rate = 0.02
epsilon = 1e-08
teacher_keep = 0.75

def adam_step(values, moment_one, moment_two, gradient):
    first_new = beta_one * moment_one.astype(jnp.float32) + (1.0 - beta_one) * gradient
    second_new = beta_two * moment_two.astype(jnp.float32) + (1.0 - beta_two) * gradient * gradient
    values_new = values.astype(jnp.float32) - learn_rate * first_new / (jnp.sqrt(second_new) + epsilon)
    return (values_new, first_new, second_new)

def reference(student_hidden, out_cotangent, student_branch, layer_scale, scale_first, scale_second, student_weight, first_moment, second_moment, teacher_weight, teacher_scale, teacher_hidden, teacher_input):
    cotangent = out_cotangent.astype(jnp.float32)
    scaled = (cotangent * layer_scale).astype(jnp.bfloat16)
    weight_grad = lax.dot_general(student_hidden, scaled, (((0,), (0,)), ((), ())), preferred_element_type=jnp.float32)
    scale_grad = lax.optimization_barrier(jnp.sum(cotangent * student_branch.astype(jnp.float32), axis=0))
    weight_new, first_new, second_new = adam_step(student_weight, first_moment, second_moment, weight_grad)
    scale_new, scale_first_new, scale_second_new = adam_step(layer_scale, scale_first, scale_second, scale_grad)
    teacher_new = (teacher_keep * teacher_weight.astype(jnp.float32) + (1.0 - teacher_keep) * weight_new).astype(jnp.bfloat16)
    teacher_scale_new = teacher_keep * teacher_scale + (1.0 - teacher_keep) * scale_new
    projected = jnp.dot(teacher_hidden, teacher_new, preferred_element_type=jnp.float32)
    teacher_out = (teacher_input.astype(jnp.float32) + teacher_scale_new * projected).astype(jnp.bfloat16)
    return (weight_new.astype(jnp.bfloat16), first_new.astype(jnp.bfloat16), second_new.astype(jnp.bfloat16), teacher_new, scale_new, scale_first_new, scale_second_new, teacher_scale_new, teacher_out)
```

```python
import jax
import jax.numpy as jnp
from jax import lax
from jax.sharding import PartitionSpec as P

beta_one = 0.9
beta_two = 0.95
learn_rate = 0.02
epsilon = 1e-08
teacher_keep = 0.75

BOTH = ("fsdp", "rep")


def adam_step(values, moment_one, moment_two, gradient):
    first_new = beta_one * moment_one.astype(jnp.float32) + (1.0 - beta_one) * gradient
    second_new = beta_two * moment_two.astype(jnp.float32) + (1.0 - beta_two) * gradient * gradient
    values_new = values.astype(jnp.float32) - learn_rate * first_new / (
        jnp.sqrt(second_new) + epsilon
    )
    return (values_new, first_new, second_new)


def token_fold(arrived, portion):
    return lax.dot_general(
        arrived, portion, (((0,), (0,)), ((), ())), preferred_element_type=jnp.float32
    )


def swap_fsdp(value, flip):
    count = lax.axis_size("fsdp")
    return lax.ppermute(value, "fsdp", [(i, i ^ flip) for i in range(count)])


def swap_rep(value, flip):
    count = lax.axis_size("rep")
    return lax.ppermute(value, "rep", [(i, i ^ flip) for i in range(count)])


def gather_chips(value, chips):
    rows = value.shape[0]
    if chips == 4 and rows % 32 == 0:
        along_x = swap_fsdp(value, 2)
        along_y = swap_fsdp(value, 4)
        half = rows // 2
        corner = [swap_fsdp(along_x[:half], 4), swap_fsdp(along_y[half:], 2)]
        return [[value], [along_x], [along_y], corner]
    return [[value]] + [[swap_fsdp(value, 2 * j)] for j in range(1, chips)]


def all_sum(value):
    flip = 1
    while flip < lax.axis_size("rep"):
        value = value + swap_rep(value, flip)
        flip *= 2
    flip = 1
    while flip < lax.axis_size("fsdp"):
        value = value + swap_fsdp(value, flip)
        flip *= 2
    return value


def shards(
    student_hidden,
    out_cotangent,
    student_branch,
    layer_scale,
    scale_first,
    scale_second,
    student_weight,
    first_moment,
    second_moment,
    teacher_weight,
    teacher_scale,
    teacher_hidden,
    teacher_input,
):
    fsdp_count = lax.axis_size("fsdp")
    rep_count = lax.axis_size("rep")
    chips = fsdp_count // 2
    own_rows = student_weight.shape[0]
    width = rep_count * own_rows
    me = lax.axis_index("fsdp")
    my_rep = lax.axis_index("rep")

    def columns(array, flip):
        return lax.dynamic_slice_in_dim(array, (me ^ flip) * width, width, 1)

    cotangent = out_cotangent.astype(jnp.float32)
    scale_grad = all_sum(jnp.sum(cotangent * student_branch.astype(jnp.float32), axis=0))
    scale_new, scale_first_new, scale_second_new = adam_step(
        layer_scale, scale_first, scale_second, scale_grad
    )
    teacher_scale_new = teacher_keep * teacher_scale + (1.0 - teacher_keep) * scale_new

    scaled = (cotangent * layer_scale).astype(jnp.bfloat16)
    scaled_of = [jnp.concatenate(b, 0) if len(b) > 1 else b[0] for b in gather_chips(scaled, chips)]
    partial_term = None
    for j in range(chips):
        sent = jnp.concatenate([columns(student_hidden, 2 * j), columns(student_hidden, 2 * j + 1)], 1)
        arrived = swap_fsdp(sent, 2 * j) if j else sent
        term = token_fold(arrived, scaled_of[j])
        partial_term = term if partial_term is None else partial_term + term
    pair = partial_term[:width] + swap_fsdp(partial_term[width:], 1)

    def rows_of(array, flip):
        return lax.dynamic_slice_in_dim(array, (my_rep ^ flip) * own_rows, own_rows, 0)

    gradient = rows_of(pair, 0)
    for j in range(1, rep_count):
        gradient = gradient + swap_rep(rows_of(pair, j).astype(jnp.bfloat16), j).astype(jnp.float32)
    weight_new, first_new, second_new = adam_step(
        student_weight, first_moment, second_moment, gradient
    )
    teacher_rows = (
        teacher_keep * rows_of(teacher_weight, 0).astype(jnp.float32)
        + (1.0 - teacher_keep) * weight_new
    ).astype(jnp.bfloat16)
    teacher_shard = jnp.zeros((width,) + teacher_rows.shape[1:], jnp.bfloat16)
    for j in range(rep_count):
        piece = swap_rep(teacher_rows, j) if j else teacher_rows
        teacher_shard = lax.dynamic_update_slice_in_dim(
            teacher_shard, piece, (my_rep ^ j) * own_rows, 0
        )
    projected = None
    for j, blocks in enumerate(gather_chips(teacher_shard, chips)):
        low, high = columns(teacher_hidden, 2 * j), columns(teacher_hidden, 2 * j + 1)
        start = 0
        for block in blocks:
            stop = start + block.shape[0]
            for hidden, weights in ((low, block), (high, swap_fsdp(block, 1))):
                term = jnp.dot(hidden[:, start:stop], weights, preferred_element_type=jnp.float32)
                projected = term if projected is None else projected + term
            start = stop
    teacher_out = (teacher_input.astype(jnp.float32) + teacher_scale_new * projected).astype(
        jnp.bfloat16
    )
    return (
        weight_new.astype(jnp.bfloat16),
        first_new.astype(jnp.bfloat16),
        second_new.astype(jnp.bfloat16),
        teacher_shard,
        scale_new,
        scale_first_new,
        scale_second_new,
        teacher_scale_new,
        teacher_out,
    )


def solution(mesh):
    in_specs = (
        P(("fsdp", "rep"), None),
        P(("fsdp", "rep"), None),
        P(("fsdp", "rep"), None),
        P(),
        P(),
        P(),
        P(("fsdp", "rep"), None),
        P(("fsdp", "rep"), None),
        P(("fsdp", "rep"), None),
        P("fsdp", None),
        P(),
        P(("fsdp", "rep"), None),
        P(("fsdp", "rep"), None),
    )
    out_specs = (
        P(("fsdp", "rep"), None),
        P(("fsdp", "rep"), None),
        P(("fsdp", "rep"), None),
        P("fsdp", None),
        P(),
        P(),
        P(),
        P(),
        P(("fsdp", "rep"), None),
    )
    return jax.shard_map(shards, mesh=mesh, in_specs=in_specs, out_specs=out_specs, check_vma=False)
```

```python
import jax
import jax.numpy as jnp
from jax import lax
from jax.experimental import pallas as pl
from jax.experimental.pallas import tpu as pltpu
from jax.sharding import PartitionSpec as P

beta_one = 0.9
beta_two = 0.95
learn_rate = 0.02
epsilon = 1e-08
teacher_keep = 0.75

BOTH = ("fsdp", "rep")


def adam_step(values, moment_one, moment_two, gradient):
    first_new = beta_one * moment_one.astype(jnp.float32) + (1.0 - beta_one) * gradient
    second_new = beta_two * moment_two.astype(jnp.float32) + (1.0 - beta_two) * gradient * gradient
    values_new = values.astype(jnp.float32) - learn_rate * first_new / (
        jnp.sqrt(second_new) + epsilon
    )
    return (values_new, first_new, second_new)


def token_fold(arrived, portion):
    return lax.dot_general(
        arrived, portion, (((0,), (0,)), ((), ())), preferred_element_type=jnp.float32
    )


def swap_fsdp(value, flip):
    count = lax.axis_size("fsdp")
    return lax.ppermute(value, "fsdp", [(i, i ^ flip) for i in range(count)])


def swap_rep(value, flip):
    count = lax.axis_size("rep")
    return lax.ppermute(value, "rep", [(i, i ^ flip) for i in range(count)])


def gather_chips(value, chips):
    rows = value.shape[0]
    if chips == 4 and rows % 32 == 0:
        along_x = swap_fsdp(value, 2)
        along_y = swap_fsdp(value, 4)
        half = rows // 2
        corner = [swap_fsdp(along_x[:half], 4), swap_fsdp(along_y[half:], 2)]
        return [[value], [along_x], [along_y], corner]
    return [[value]] + [[swap_fsdp(value, 2 * j)] for j in range(1, chips)]


def all_sum(value):
    flip = 1
    while flip < lax.axis_size("rep"):
        value = value + swap_rep(value, flip)
        flip *= 2
    flip = 1
    while flip < lax.axis_size("fsdp"):
        value = value + swap_fsdp(value, flip)
        flip *= 2
    return value


def general_shards(
    student_hidden,
    out_cotangent,
    student_branch,
    layer_scale,
    scale_first,
    scale_second,
    student_weight,
    first_moment,
    second_moment,
    teacher_weight,
    teacher_scale,
    teacher_hidden,
    teacher_input,
):
    fsdp_count = lax.axis_size("fsdp")
    rep_count = lax.axis_size("rep")
    chips = fsdp_count // 2
    own_rows = student_weight.shape[0]
    width = rep_count * own_rows
    me = lax.axis_index("fsdp")
    my_rep = lax.axis_index("rep")

    def columns(array, flip):
        return lax.dynamic_slice_in_dim(array, (me ^ flip) * width, width, 1)

    cotangent = out_cotangent.astype(jnp.float32)
    scale_grad = all_sum(jnp.sum(cotangent * student_branch.astype(jnp.float32), axis=0))
    scale_new, scale_first_new, scale_second_new = adam_step(
        layer_scale, scale_first, scale_second, scale_grad
    )
    teacher_scale_new = teacher_keep * teacher_scale + (1.0 - teacher_keep) * scale_new

    scaled = (cotangent * layer_scale).astype(jnp.bfloat16)
    scaled_of = [jnp.concatenate(b, 0) if len(b) > 1 else b[0] for b in gather_chips(scaled, chips)]
    partial_term = None
    for j in range(chips):
        sent = jnp.concatenate([columns(student_hidden, 2 * j), columns(student_hidden, 2 * j + 1)], 1)
        arrived = swap_fsdp(sent, 2 * j) if j else sent
        term = token_fold(arrived, scaled_of[j])
        partial_term = term if partial_term is None else partial_term + term
    pair = partial_term[:width] + swap_fsdp(partial_term[width:], 1)

    def rows_of(array, flip):
        return lax.dynamic_slice_in_dim(array, (my_rep ^ flip) * own_rows, own_rows, 0)

    gradient = rows_of(pair, 0)
    for j in range(1, rep_count):
        gradient = gradient + swap_rep(rows_of(pair, j).astype(jnp.bfloat16), j).astype(jnp.float32)
    weight_new, first_new, second_new = adam_step(
        student_weight, first_moment, second_moment, gradient
    )
    teacher_rows = (
        teacher_keep * rows_of(teacher_weight, 0).astype(jnp.float32)
        + (1.0 - teacher_keep) * weight_new
    ).astype(jnp.bfloat16)
    teacher_shard = jnp.zeros((width,) + teacher_rows.shape[1:], jnp.bfloat16)
    for j in range(rep_count):
        piece = swap_rep(teacher_rows, j) if j else teacher_rows
        teacher_shard = lax.dynamic_update_slice_in_dim(
            teacher_shard, piece, (my_rep ^ j) * own_rows, 0
        )
    projected = None
    for j, blocks in enumerate(gather_chips(teacher_shard, chips)):
        low, high = columns(teacher_hidden, 2 * j), columns(teacher_hidden, 2 * j + 1)
        start = 0
        for block in blocks:
            stop = start + block.shape[0]
            for hidden, weights in ((low, block), (high, swap_fsdp(block, 1))):
                term = jnp.dot(hidden[:, start:stop], weights, preferred_element_type=jnp.float32)
                projected = term if projected is None else projected + term
            start = stop
    teacher_out = (teacher_input.astype(jnp.float32) + teacher_scale_new * projected).astype(
        jnp.bfloat16
    )
    return (
        weight_new.astype(jnp.bfloat16),
        first_new.astype(jnp.bfloat16),
        second_new.astype(jnp.bfloat16),
        teacher_shard,
        scale_new,
        scale_first_new,
        scale_second_new,
        teacher_scale_new,
        teacher_out,
    )


def after(value, *others):
    return lax.optimization_barrier((value,) + others)[0]


MIB = 1024 * 1024
VMEM = pl.BlockSpec(memory_space=pltpu.VMEM)
SMEM = pl.BlockSpec(memory_space=pltpu.SMEM)


def three_parts(value):
    high = lax.reduce_precision(value, 8, 7)
    rest = value - high
    mid = lax.reduce_precision(rest, 8, 7)
    return [high, mid, rest - mid]


def split_kernel(place, keep, arrived, own, *outgoing):
    rows = own.shape[0]
    for j in range(len(outgoing) + 1):
        at = pl.ds(pl.multiple_of((place[0] ^ j) * rows, 32), rows)
        total = keep[at, :] + arrived[at, :]
        if j:
            outgoing[j - 1][...] = total.astype(jnp.bfloat16)
        else:
            own[...] = total


def split_rows(place, keep, arrived, rows, count):
    width = keep.shape[1]
    return pl.pallas_call(
        split_kernel,
        out_shape=[jax.ShapeDtypeStruct((rows, width), jnp.float32)]
        + [jax.ShapeDtypeStruct((rows, width), jnp.bfloat16)] * (count - 1),
        in_specs=[SMEM, VMEM, VMEM],
        out_specs=[VMEM] * count,
        compiler_params=pltpu.CompilerParams(vmem_limit_bytes=24 * MIB),
        cost_estimate=pl.CostEstimate(
            flops=keep.size, bytes_accessed=11 * keep.size, transcendentals=0
        ),
        name="split_rows",
    )(place, keep, arrived)


def update_kernel(place, own, one, two, three, weight, first, second, teacher, *outs):
    new_weight, new_first, new_second, sent = outs
    rows = own.shape[0]
    gradient = own[...] + one[...].astype(jnp.float32)
    gradient = gradient + two[...].astype(jnp.float32) + three[...].astype(jnp.float32)
    weight_new, first_new, second_new = adam_step(
        weight[...], first[...], second[...], gradient
    )
    new_weight[...] = weight_new.astype(jnp.bfloat16)
    new_first[...] = first_new.astype(jnp.bfloat16)
    new_second[...] = second_new.astype(jnp.bfloat16)
    held = teacher[pl.ds(pl.multiple_of(place[0] * rows, 32), rows), :].astype(jnp.float32)
    sent[...] = (teacher_keep * held + (1.0 - teacher_keep) * weight_new).astype(jnp.bfloat16)


def update_rows(place, own, arrived, weight, first, second, teacher):
    rows, width = own.shape
    stored = jax.ShapeDtypeStruct((rows, width), jnp.bfloat16)
    return pl.pallas_call(
        update_kernel,
        out_shape=[stored] * 4,
        in_specs=[SMEM] + [VMEM] * 8,
        out_specs=[VMEM] * 4,
        compiler_params=pltpu.CompilerParams(vmem_limit_bytes=24 * MIB),
        cost_estimate=pl.CostEstimate(
            flops=20 * own.size, bytes_accessed=30 * own.size, transcendentals=2 * own.size
        ),
        name="update_rows",
    )(place, own, *arrived, weight, first, second, teacher)


def block_shards(
    student_hidden,
    out_cotangent,
    student_branch,
    layer_scale,
    scale_first,
    scale_second,
    student_weight,
    first_moment,
    second_moment,
    teacher_weight,
    teacher_scale,
    teacher_hidden,
    teacher_input,
):
    rep_count = 4
    tokens = student_hidden.shape[0]
    own_rows, model_width = student_weight.shape
    width = rep_count * own_rows
    pair_rows = 2 * own_rows
    me = lax.axis_index("fsdp")
    my_rep = lax.axis_index("rep")
    place = my_rep.astype(jnp.int32).reshape(1)

    def columns(array, flip):
        return lax.dynamic_slice_in_dim(array, (me ^ flip) * width, width, 1)

    cot_x, cot_y = swap_fsdp(out_cotangent, 2), swap_fsdp(out_cotangent, 4)
    share = jnp.sum(
        out_cotangent.astype(jnp.float32) * student_branch.astype(jnp.float32), axis=0
    )
    tail = jnp.stack(three_parts(share)).astype(jnp.bfloat16)
    tail = jnp.pad(tail, ((0, 8 - 3), (0, 0)))
    hidden_of = [jnp.concatenate([columns(student_hidden, 0), columns(student_hidden, 1)], 1)]
    for flip in (2, 4, 6):
        sent = jnp.concatenate([columns(student_hidden, flip), columns(student_hidden, flip + 1)], 1)
        hidden_of.append(swap_fsdp(jnp.concatenate([sent, tail], 0), flip))
    half = tokens // 2
    corner = [swap_fsdp(cot_x[:half], 4), swap_fsdp(cot_y[half:], 2)]
    cotangents = [[out_cotangent], [cot_x], [cot_y], corner]
    for hidden in hidden_of[1:]:
        share = share + jnp.sum(hidden[tokens : tokens + 3].astype(jnp.float32), axis=0)

    def scale_it(block):
        scaled = (block.astype(jnp.float32) * layer_scale).astype(jnp.bfloat16)
        return lax.optimization_barrier(scaled)

    keep = send = None
    for hidden, blocks in zip(hidden_of, cotangents):
        start = 0
        for block in blocks:
            stop = start + block.shape[0]
            scaled = scale_it(block)
            term = token_fold(hidden[start:stop, width:], scaled)
            send = term if send is None else send + term
            term = token_fold(hidden[start:stop, :width], scaled)
            keep = term if keep is None else keep + term
            start = stop
    share = share + swap_fsdp(share, 1)
    own, *outgoing = split_rows(place, keep, swap_fsdp(send, 1), own_rows, rep_count)
    arrived = [swap_rep(piece, j + 1) for j, piece in enumerate(outgoing)]
    new_weight, new_first, new_second, sent_rows = update_rows(
        place,
        own,
        arrived,
        student_weight,
        first_moment,
        second_moment,
        teacher_weight,
    )

    teacher_shard = lax.all_gather(sent_rows, "rep", axis=0, tiled=True)
    share = sum([swap_rep(share, j) for j in range(1, rep_count)], share)
    scale_new, scale_first_new, scale_second_new = adam_step(
        layer_scale, scale_first, scale_second, share
    )
    teacher_scale_new = teacher_keep * teacher_scale + (1.0 - teacher_keep) * scale_new

    along_x, along_y = swap_fsdp(teacher_shard, 2), swap_fsdp(teacher_shard, 4)
    corner_x = swap_fsdp(along_x[:pair_rows], 4)
    corner_y = swap_fsdp(along_y[pair_rows:], 2)
    held = [(teacher_shard, 0, 0), (along_x, 2, 0), (along_y, 4, 0)]
    held += [(corner_x, 6, 0), (corner_y, 6, pair_rows)]
    projected = None
    for block, flip, start in held:
        for weights, f in ((block, flip), (swap_fsdp(block, 1), flip + 1)):
            units = columns(teacher_hidden, f)[:, start : start + block.shape[0]]
            term = jnp.dot(units, weights, preferred_element_type=jnp.float32)
            projected = term if projected is None else projected + term
    teacher_out = (teacher_input.astype(jnp.float32) + teacher_scale_new * projected).astype(
        jnp.bfloat16
    )
    return (
        new_weight,
        new_first,
        new_second,
        teacher_shard,
        scale_new,
        scale_first_new,
        scale_second_new,
        teacher_scale_new,
        teacher_out,
    )


def shards(*args):
    hidden, weight = args[0], args[6]
    rows, model_width = weight.shape
    fits = (
        lax.axis_size("fsdp") == 8
        and lax.axis_size("rep") == 4
        and rows % 32 == 0
        and hidden.shape[0] % 32 == 0
        and 8 * rows == model_width
        and model_width % 256 == 0
    )
    return block_shards(*args) if fits else general_shards(*args)


def solution(mesh):
    in_specs = (
        P(("fsdp", "rep"), None),
        P(("fsdp", "rep"), None),
        P(("fsdp", "rep"), None),
        P(),
        P(),
        P(),
        P(("fsdp", "rep"), None),
        P(("fsdp", "rep"), None),
        P(("fsdp", "rep"), None),
        P("fsdp", None),
        P(),
        P(("fsdp", "rep"), None),
        P(("fsdp", "rep"), None),
    )
    out_specs = (
        P(("fsdp", "rep"), None),
        P(("fsdp", "rep"), None),
        P(("fsdp", "rep"), None),
        P("fsdp", None),
        P(),
        P(),
        P(),
        P(),
        P(("fsdp", "rep"), None),
    )
    return jax.shard_map(shards, mesh=mesh, in_specs=in_specs, out_specs=out_specs, check_vma=False)
```

```python
import jax
import jax.numpy as jnp
from jax import lax
from jax.experimental import pallas as pl
from jax.experimental.pallas import tpu as pltpu
from jax.sharding import PartitionSpec as P

beta_one = 0.9
beta_two = 0.95
learn_rate = 0.02
epsilon = 1e-08
teacher_keep = 0.75

BOTH = ("fsdp", "rep")


def adam_step(values, moment_one, moment_two, gradient):
    first_new = beta_one * moment_one.astype(jnp.float32) + (1.0 - beta_one) * gradient
    second_new = beta_two * moment_two.astype(jnp.float32) + (1.0 - beta_two) * gradient * gradient
    values_new = values.astype(jnp.float32) - learn_rate * first_new / (
        jnp.sqrt(second_new) + epsilon
    )
    return (values_new, first_new, second_new)


def token_fold(arrived, portion):
    return lax.dot_general(
        arrived, portion, (((0,), (0,)), ((), ())), preferred_element_type=jnp.float32
    )


def swap_fsdp(value, flip):
    count = lax.axis_size("fsdp")
    return lax.ppermute(value, "fsdp", [(i, i ^ flip) for i in range(count)])


def swap_rep(value, flip):
    count = lax.axis_size("rep")
    return lax.ppermute(value, "rep", [(i, i ^ flip) for i in range(count)])


def gather_chips(value, chips):
    rows = value.shape[0]
    if chips == 4 and rows % 32 == 0:
        along_x = swap_fsdp(value, 2)
        along_y = swap_fsdp(value, 4)
        half = rows // 2
        corner = [swap_fsdp(along_x[:half], 4), swap_fsdp(along_y[half:], 2)]
        return [[value], [along_x], [along_y], corner]
    return [[value]] + [[swap_fsdp(value, 2 * j)] for j in range(1, chips)]


def all_sum(value):
    flip = 1
    while flip < lax.axis_size("rep"):
        value = value + swap_rep(value, flip)
        flip *= 2
    flip = 1
    while flip < lax.axis_size("fsdp"):
        value = value + swap_fsdp(value, flip)
        flip *= 2
    return value


def general_shards(
    student_hidden,
    out_cotangent,
    student_branch,
    layer_scale,
    scale_first,
    scale_second,
    student_weight,
    first_moment,
    second_moment,
    teacher_weight,
    teacher_scale,
    teacher_hidden,
    teacher_input,
):
    fsdp_count = lax.axis_size("fsdp")
    rep_count = lax.axis_size("rep")
    chips = fsdp_count // 2
    own_rows = student_weight.shape[0]
    width = rep_count * own_rows
    me = lax.axis_index("fsdp")
    my_rep = lax.axis_index("rep")

    def columns(array, flip):
        return lax.dynamic_slice_in_dim(array, (me ^ flip) * width, width, 1)

    cotangent = out_cotangent.astype(jnp.float32)
    scale_grad = all_sum(jnp.sum(cotangent * student_branch.astype(jnp.float32), axis=0))
    scale_new, scale_first_new, scale_second_new = adam_step(
        layer_scale, scale_first, scale_second, scale_grad
    )
    teacher_scale_new = teacher_keep * teacher_scale + (1.0 - teacher_keep) * scale_new

    scaled = (cotangent * layer_scale).astype(jnp.bfloat16)
    scaled_of = [jnp.concatenate(b, 0) if len(b) > 1 else b[0] for b in gather_chips(scaled, chips)]
    partial_term = None
    for j in range(chips):
        sent = jnp.concatenate([columns(student_hidden, 2 * j), columns(student_hidden, 2 * j + 1)], 1)
        arrived = swap_fsdp(sent, 2 * j) if j else sent
        term = token_fold(arrived, scaled_of[j])
        partial_term = term if partial_term is None else partial_term + term
    pair = partial_term[:width] + swap_fsdp(partial_term[width:], 1)

    def rows_of(array, flip):
        return lax.dynamic_slice_in_dim(array, (my_rep ^ flip) * own_rows, own_rows, 0)

    gradient = rows_of(pair, 0)
    for j in range(1, rep_count):
        gradient = gradient + swap_rep(rows_of(pair, j).astype(jnp.bfloat16), j).astype(jnp.float32)
    weight_new, first_new, second_new = adam_step(
        student_weight, first_moment, second_moment, gradient
    )
    teacher_rows = (
        teacher_keep * rows_of(teacher_weight, 0).astype(jnp.float32)
        + (1.0 - teacher_keep) * weight_new
    ).astype(jnp.bfloat16)
    teacher_shard = jnp.zeros((width,) + teacher_rows.shape[1:], jnp.bfloat16)
    for j in range(rep_count):
        piece = swap_rep(teacher_rows, j) if j else teacher_rows
        teacher_shard = lax.dynamic_update_slice_in_dim(
            teacher_shard, piece, (my_rep ^ j) * own_rows, 0
        )
    projected = None
    for j, blocks in enumerate(gather_chips(teacher_shard, chips)):
        low, high = columns(teacher_hidden, 2 * j), columns(teacher_hidden, 2 * j + 1)
        start = 0
        for block in blocks:
            stop = start + block.shape[0]
            for hidden, weights in ((low, block), (high, swap_fsdp(block, 1))):
                term = jnp.dot(hidden[:, start:stop], weights, preferred_element_type=jnp.float32)
                projected = term if projected is None else projected + term
            start = stop
    teacher_out = (teacher_input.astype(jnp.float32) + teacher_scale_new * projected).astype(
        jnp.bfloat16
    )
    return (
        weight_new.astype(jnp.bfloat16),
        first_new.astype(jnp.bfloat16),
        second_new.astype(jnp.bfloat16),
        teacher_shard,
        scale_new,
        scale_first_new,
        scale_second_new,
        teacher_scale_new,
        teacher_out,
    )


def after(value, *others):
    return lax.optimization_barrier((value,) + others)[0]


MIB = 1024 * 1024
VMEM = pl.BlockSpec(memory_space=pltpu.VMEM)
SMEM = pl.BlockSpec(memory_space=pltpu.SMEM)


def three_parts(value):
    high = lax.reduce_precision(value, 8, 7)
    rest = value - high
    mid = lax.reduce_precision(rest, 8, 7)
    return [high, mid, rest - mid]


def fold_kernel(scale, *refs):
    hidden, cotangent, (keep, send) = refs[:3], refs[3:6], refs[6:]
    width = keep.shape[0]
    tokens = cotangent[0].shape[0]
    parts = [None, None]
    for h, c in zip(hidden, cotangent):
        scaled = (c[...].astype(jnp.float32) * scale[...]).astype(jnp.bfloat16)
        for k in range(2):
            term = token_fold(h[:tokens, k * width : (k + 1) * width], scaled)
            parts[k] = term if parts[k] is None else parts[k] + term
    keep[...] = parts[0]
    send[...] = parts[1]


def fold_tokens(scale, hidden, cotangent, width):
    model_width = cotangent[0].shape[1]
    total = jax.ShapeDtypeStruct((width, model_width), jnp.float32)
    return pl.pallas_call(
        fold_kernel,
        out_shape=[total, total],
        in_specs=[VMEM] * 7,
        out_specs=[VMEM] * 2,
        compiler_params=pltpu.CompilerParams(vmem_limit_bytes=24 * MIB),
        cost_estimate=pl.CostEstimate(
            flops=12 * cotangent[0].size * width,
            bytes_accessed=4 * model_width * width + 12 * cotangent[0].size,
            transcendentals=0,
        ),
        name="fold_tokens",
    )(scale.reshape(1, -1), *hidden, *cotangent)


def split_kernel(place, keep, arrived, own, *outgoing):
    rows = own.shape[0]
    for j in range(len(outgoing) + 1):
        at = pl.ds(pl.multiple_of((place[0] ^ j) * rows, 32), rows)
        total = keep[at, :] + arrived[at, :]
        if j:
            outgoing[j - 1][...] = total.astype(jnp.bfloat16)
        else:
            own[...] = total


def split_rows(place, keep, arrived, rows, count):
    width = keep.shape[1]
    return pl.pallas_call(
        split_kernel,
        out_shape=[jax.ShapeDtypeStruct((rows, width), jnp.float32)]
        + [jax.ShapeDtypeStruct((rows, width), jnp.bfloat16)] * (count - 1),
        in_specs=[SMEM, VMEM, VMEM],
        out_specs=[VMEM] * count,
        compiler_params=pltpu.CompilerParams(vmem_limit_bytes=24 * MIB),
        cost_estimate=pl.CostEstimate(
            flops=keep.size, bytes_accessed=11 * keep.size, transcendentals=0
        ),
        name="split_rows",
    )(place, keep, arrived)


def update_kernel(place, own, one, two, three, weight, first, second, teacher, *outs):
    new_weight, new_first, new_second, sent = outs
    rows = own.shape[0]
    gradient = own[...] + one[...].astype(jnp.float32)
    gradient = gradient + two[...].astype(jnp.float32) + three[...].astype(jnp.float32)
    weight_new, first_new, second_new = adam_step(
        weight[...], first[...], second[...], gradient
    )
    new_weight[...] = weight_new.astype(jnp.bfloat16)
    new_first[...] = first_new.astype(jnp.bfloat16)
    new_second[...] = second_new.astype(jnp.bfloat16)
    held = teacher[pl.ds(pl.multiple_of(place[0] * rows, 32), rows), :].astype(jnp.float32)
    sent[...] = (teacher_keep * held + (1.0 - teacher_keep) * weight_new).astype(jnp.bfloat16)


def update_rows(place, own, arrived, weight, first, second, teacher):
    rows, width = own.shape
    stored = jax.ShapeDtypeStruct((rows, width), jnp.bfloat16)
    return pl.pallas_call(
        update_kernel,
        out_shape=[stored] * 4,
        in_specs=[SMEM] + [VMEM] * 8,
        out_specs=[VMEM] * 4,
        compiler_params=pltpu.CompilerParams(vmem_limit_bytes=24 * MIB),
        cost_estimate=pl.CostEstimate(
            flops=20 * own.size, bytes_accessed=30 * own.size, transcendentals=2 * own.size
        ),
        name="update_rows",
    )(place, own, *arrived, weight, first, second, teacher)


def block_shards(
    student_hidden,
    out_cotangent,
    student_branch,
    layer_scale,
    scale_first,
    scale_second,
    student_weight,
    first_moment,
    second_moment,
    teacher_weight,
    teacher_scale,
    teacher_hidden,
    teacher_input,
):
    rep_count = 4
    tokens = student_hidden.shape[0]
    own_rows, model_width = student_weight.shape
    width = rep_count * own_rows
    pair_rows = 2 * own_rows
    me = lax.axis_index("fsdp")
    my_rep = lax.axis_index("rep")
    place = my_rep.astype(jnp.int32).reshape(1)

    def columns(array, flip):
        return lax.dynamic_slice_in_dim(array, (me ^ flip) * width, width, 1)

    cot_x, cot_y = swap_fsdp(out_cotangent, 2), swap_fsdp(out_cotangent, 4)
    share = jnp.sum(
        out_cotangent.astype(jnp.float32) * student_branch.astype(jnp.float32), axis=0
    )
    tail = jnp.stack(three_parts(share)).astype(jnp.bfloat16)
    tail = jnp.pad(tail, ((0, 8 - 3), (0, 0)))
    hidden_of = [jnp.concatenate([columns(student_hidden, 0), columns(student_hidden, 1)], 1)]
    for flip in (2, 4, 6):
        sent = jnp.concatenate([columns(student_hidden, flip), columns(student_hidden, flip + 1)], 1)
        hidden_of.append(swap_fsdp(jnp.concatenate([sent, tail], 0), flip))
    half = tokens // 2
    corner = [swap_fsdp(cot_x[:half], 4), swap_fsdp(cot_y[half:], 2)]
    for hidden in hidden_of[1:]:
        share = share + jnp.sum(hidden[tokens : tokens + 3].astype(jnp.float32), axis=0)

    def scale_it(block):
        scaled = (block.astype(jnp.float32) * layer_scale).astype(jnp.bfloat16)
        return lax.optimization_barrier(scaled)

    keep, send = fold_tokens(layer_scale, hidden_of[:3], [out_cotangent, cot_x, cot_y], width)
    scaled = scale_it(jnp.concatenate(corner, 0))
    far = hidden_of[3][:tokens]
    send = send + token_fold(far[:, width:], scaled)
    keep = keep + token_fold(far[:, :width], scaled)
    share = share + swap_fsdp(share, 1)
    own, *outgoing = split_rows(place, keep, swap_fsdp(send, 1), own_rows, rep_count)
    arrived = [swap_rep(piece, j + 1) for j, piece in enumerate(outgoing)]
    new_weight, new_first, new_second, sent_rows = update_rows(
        place,
        own,
        arrived,
        student_weight,
        first_moment,
        second_moment,
        teacher_weight,
    )

    teacher_shard = lax.all_gather(sent_rows, "rep", axis=0, tiled=True)
    share = sum([swap_rep(share, j) for j in range(1, rep_count)], share)
    scale_new, scale_first_new, scale_second_new = adam_step(
        layer_scale, scale_first, scale_second, share
    )
    teacher_scale_new = teacher_keep * teacher_scale + (1.0 - teacher_keep) * scale_new

    along_x, along_y = swap_fsdp(teacher_shard, 2), swap_fsdp(teacher_shard, 4)
    corner_x = swap_fsdp(along_x[:pair_rows], 4)
    corner_y = swap_fsdp(along_y[pair_rows:], 2)

    def terms(block, flip, start):
        total = None
        for weights, f in ((block, flip), (swap_fsdp(block, 1), flip + 1)):
            units = columns(teacher_hidden, f)[:, start : start + block.shape[0]]
            term = jnp.dot(units, weights, preferred_element_type=jnp.float32)
            total = term if total is None else total + term
        return total

    near = terms(teacher_shard, 0, 0) + terms(along_x, 2, 0) + terms(along_y, 4, 0)
    near = teacher_input.astype(jnp.float32) + teacher_scale_new * near
    stored_shard = jnp.where(me >= 0, teacher_shard, jnp.zeros_like(teacher_shard))
    near, stored_shard = lax.optimization_barrier((near, stored_shard))
    far = terms(corner_x, 6, 0) + terms(corner_y, 6, pair_rows)
    teacher_out = (near + teacher_scale_new * far).astype(jnp.bfloat16)
    return (
        new_weight,
        new_first,
        new_second,
        stored_shard,
        scale_new,
        scale_first_new,
        scale_second_new,
        teacher_scale_new,
        teacher_out,
    )


def shards(*args):
    hidden, weight = args[0], args[6]
    rows, model_width = weight.shape
    fits = (
        lax.axis_size("fsdp") == 8
        and lax.axis_size("rep") == 4
        and rows % 32 == 0
        and hidden.shape[0] % 32 == 0
        and 8 * rows == model_width
        and model_width % 256 == 0
    )
    return block_shards(*args) if fits else general_shards(*args)


def solution(mesh):
    in_specs = (
        P(("fsdp", "rep"), None),
        P(("fsdp", "rep"), None),
        P(("fsdp", "rep"), None),
        P(),
        P(),
        P(),
        P(("fsdp", "rep"), None),
        P(("fsdp", "rep"), None),
        P(("fsdp", "rep"), None),
        P("fsdp", None),
        P(),
        P(("fsdp", "rep"), None),
        P(("fsdp", "rep"), None),
    )
    out_specs = (
        P(("fsdp", "rep"), None),
        P(("fsdp", "rep"), None),
        P(("fsdp", "rep"), None),
        P("fsdp", None),
        P(),
        P(),
        P(),
        P(),
        P(("fsdp", "rep"), None),
    )
    return jax.shard_map(shards, mesh=mesh, in_specs=in_specs, out_specs=out_specs, check_vma=False)
```

```python
import jax
import jax.numpy as jnp
from jax import lax
from jax.experimental import pallas as pl
from jax.experimental.pallas import tpu as pltpu
from jax.sharding import PartitionSpec as P

beta_one = 0.9
beta_two = 0.95
learn_rate = 0.02
epsilon = 1e-08
teacher_keep = 0.75

BOTH = ("fsdp", "rep")


def adam_step(values, moment_one, moment_two, gradient):
    first_new = beta_one * moment_one.astype(jnp.float32) + (1.0 - beta_one) * gradient
    second_new = beta_two * moment_two.astype(jnp.float32) + (1.0 - beta_two) * gradient * gradient
    values_new = values.astype(jnp.float32) - learn_rate * first_new / (
        jnp.sqrt(second_new) + epsilon
    )
    return (values_new, first_new, second_new)


def token_fold(arrived, portion):
    return lax.dot_general(
        arrived, portion, (((0,), (0,)), ((), ())), preferred_element_type=jnp.float32
    )


def swap_fsdp(value, flip):
    count = lax.axis_size("fsdp")
    return lax.ppermute(value, "fsdp", [(i, i ^ flip) for i in range(count)])


def swap_rep(value, flip):
    count = lax.axis_size("rep")
    return lax.ppermute(value, "rep", [(i, i ^ flip) for i in range(count)])


def gather_chips(value, chips):
    rows = value.shape[0]
    if chips == 4 and rows % 32 == 0:
        along_x = swap_fsdp(value, 2)
        along_y = swap_fsdp(value, 4)
        half = rows // 2
        corner = [swap_fsdp(along_x[:half], 4), swap_fsdp(along_y[half:], 2)]
        return [[value], [along_x], [along_y], corner]
    return [[value]] + [[swap_fsdp(value, 2 * j)] for j in range(1, chips)]


def all_sum(value):
    flip = 1
    while flip < lax.axis_size("rep"):
        value = value + swap_rep(value, flip)
        flip *= 2
    flip = 1
    while flip < lax.axis_size("fsdp"):
        value = value + swap_fsdp(value, flip)
        flip *= 2
    return value


def general_shards(
    student_hidden,
    out_cotangent,
    student_branch,
    layer_scale,
    scale_first,
    scale_second,
    student_weight,
    first_moment,
    second_moment,
    teacher_weight,
    teacher_scale,
    teacher_hidden,
    teacher_input,
):
    fsdp_count = lax.axis_size("fsdp")
    rep_count = lax.axis_size("rep")
    chips = fsdp_count // 2
    own_rows = student_weight.shape[0]
    width = rep_count * own_rows
    me = lax.axis_index("fsdp")
    my_rep = lax.axis_index("rep")

    def columns(array, flip):
        return lax.dynamic_slice_in_dim(array, (me ^ flip) * width, width, 1)

    cotangent = out_cotangent.astype(jnp.float32)
    scale_grad = all_sum(jnp.sum(cotangent * student_branch.astype(jnp.float32), axis=0))
    scale_new, scale_first_new, scale_second_new = adam_step(
        layer_scale, scale_first, scale_second, scale_grad
    )
    teacher_scale_new = teacher_keep * teacher_scale + (1.0 - teacher_keep) * scale_new

    scaled = (cotangent * layer_scale).astype(jnp.bfloat16)
    scaled_of = [jnp.concatenate(b, 0) if len(b) > 1 else b[0] for b in gather_chips(scaled, chips)]
    partial_term = None
    for j in range(chips):
        sent = jnp.concatenate([columns(student_hidden, 2 * j), columns(student_hidden, 2 * j + 1)], 1)
        arrived = swap_fsdp(sent, 2 * j) if j else sent
        term = token_fold(arrived, scaled_of[j])
        partial_term = term if partial_term is None else partial_term + term
    pair = partial_term[:width] + swap_fsdp(partial_term[width:], 1)

    def rows_of(array, flip):
        return lax.dynamic_slice_in_dim(array, (my_rep ^ flip) * own_rows, own_rows, 0)

    gradient = rows_of(pair, 0)
    for j in range(1, rep_count):
        gradient = gradient + swap_rep(rows_of(pair, j).astype(jnp.bfloat16), j).astype(jnp.float32)
    weight_new, first_new, second_new = adam_step(
        student_weight, first_moment, second_moment, gradient
    )
    teacher_rows = (
        teacher_keep * rows_of(teacher_weight, 0).astype(jnp.float32)
        + (1.0 - teacher_keep) * weight_new
    ).astype(jnp.bfloat16)
    teacher_shard = jnp.zeros((width,) + teacher_rows.shape[1:], jnp.bfloat16)
    for j in range(rep_count):
        piece = swap_rep(teacher_rows, j) if j else teacher_rows
        teacher_shard = lax.dynamic_update_slice_in_dim(
            teacher_shard, piece, (my_rep ^ j) * own_rows, 0
        )
    projected = None
    for j, blocks in enumerate(gather_chips(teacher_shard, chips)):
        low, high = columns(teacher_hidden, 2 * j), columns(teacher_hidden, 2 * j + 1)
        start = 0
        for block in blocks:
            stop = start + block.shape[0]
            for hidden, weights in ((low, block), (high, swap_fsdp(block, 1))):
                term = jnp.dot(hidden[:, start:stop], weights, preferred_element_type=jnp.float32)
                projected = term if projected is None else projected + term
            start = stop
    teacher_out = (teacher_input.astype(jnp.float32) + teacher_scale_new * projected).astype(
        jnp.bfloat16
    )
    return (
        weight_new.astype(jnp.bfloat16),
        first_new.astype(jnp.bfloat16),
        second_new.astype(jnp.bfloat16),
        teacher_shard,
        scale_new,
        scale_first_new,
        scale_second_new,
        teacher_scale_new,
        teacher_out,
    )


def after(value, *others):
    return lax.optimization_barrier((value,) + others)[0]


MIB = 1024 * 1024
VMEM = pl.BlockSpec(memory_space=pltpu.VMEM)
SMEM = pl.BlockSpec(memory_space=pltpu.SMEM)


def three_parts(value):
    high = lax.reduce_precision(value, 8, 7)
    rest = value - high
    mid = lax.reduce_precision(rest, 8, 7)
    return [high, mid, rest - mid]


def fold_kernel(scale, *refs):
    hidden, cotangent, (keep, send) = refs[:3], refs[3:6], refs[6:]
    width = keep.shape[0]
    tokens = cotangent[0].shape[0]
    parts = [None, None]
    for h, c in zip(hidden, cotangent):
        scaled = (c[...].astype(jnp.float32) * scale[...]).astype(jnp.bfloat16)
        for k in range(2):
            term = token_fold(h[:tokens, k * width : (k + 1) * width], scaled)
            parts[k] = term if parts[k] is None else parts[k] + term
    keep[...] = parts[0]
    send[...] = parts[1]


def fold_tokens(scale, hidden, cotangent, width):
    model_width = cotangent[0].shape[1]
    total = jax.ShapeDtypeStruct((width, model_width), jnp.float32)
    return pl.pallas_call(
        fold_kernel,
        out_shape=[total, total],
        in_specs=[VMEM] * 7,
        out_specs=[VMEM] * 2,
        compiler_params=pltpu.CompilerParams(vmem_limit_bytes=24 * MIB),
        cost_estimate=pl.CostEstimate(
            flops=12 * cotangent[0].size * width,
            bytes_accessed=4 * model_width * width + 12 * cotangent[0].size,
            transcendentals=0,
        ),
        name="fold_tokens",
    )(scale.reshape(1, -1), *hidden, *cotangent)


def split_kernel(place, keep, arrived, own, *outgoing):
    rows = own.shape[0]
    for j in range(len(outgoing) + 1):
        at = pl.ds(pl.multiple_of((place[0] ^ j) * rows, 32), rows)
        total = keep[at, :] + arrived[at, :].astype(jnp.float32)
        if j:
            outgoing[j - 1][...] = total.astype(jnp.bfloat16)
        else:
            own[...] = total


def split_rows(place, keep, arrived, rows, count):
    width = keep.shape[1]
    return pl.pallas_call(
        split_kernel,
        out_shape=[jax.ShapeDtypeStruct((rows, width), jnp.float32)]
        + [jax.ShapeDtypeStruct((rows, width), jnp.bfloat16)] * (count - 1),
        in_specs=[SMEM, VMEM, VMEM],
        out_specs=[VMEM] * count,
        compiler_params=pltpu.CompilerParams(vmem_limit_bytes=24 * MIB),
        cost_estimate=pl.CostEstimate(
            flops=keep.size, bytes_accessed=11 * keep.size, transcendentals=0
        ),
        name="split_rows",
    )(place, keep, arrived)


def update_kernel(place, own, one, two, three, weight, first, second, teacher, *outs):
    new_weight, new_first, new_second, sent = outs
    rows = own.shape[0]
    gradient = own[...] + one[...].astype(jnp.float32)
    gradient = gradient + two[...].astype(jnp.float32) + three[...].astype(jnp.float32)
    weight_new, first_new, second_new = adam_step(
        weight[...], first[...], second[...], gradient
    )
    new_weight[...] = weight_new.astype(jnp.bfloat16)
    new_first[...] = first_new.astype(jnp.bfloat16)
    new_second[...] = second_new.astype(jnp.bfloat16)
    held = teacher[pl.ds(pl.multiple_of(place[0] * rows, 32), rows), :].astype(jnp.float32)
    sent[...] = (teacher_keep * held + (1.0 - teacher_keep) * weight_new).astype(jnp.bfloat16)


def update_rows(place, own, arrived, weight, first, second, teacher):
    rows, width = own.shape
    stored = jax.ShapeDtypeStruct((rows, width), jnp.bfloat16)
    return pl.pallas_call(
        update_kernel,
        out_shape=[stored] * 4,
        in_specs=[SMEM] + [VMEM] * 8,
        out_specs=[VMEM] * 4,
        compiler_params=pltpu.CompilerParams(vmem_limit_bytes=24 * MIB),
        cost_estimate=pl.CostEstimate(
            flops=20 * own.size, bytes_accessed=30 * own.size, transcendentals=2 * own.size
        ),
        name="update_rows",
    )(place, own, *arrived, weight, first, second, teacher)


def block_shards(
    student_hidden,
    out_cotangent,
    student_branch,
    layer_scale,
    scale_first,
    scale_second,
    student_weight,
    first_moment,
    second_moment,
    teacher_weight,
    teacher_scale,
    teacher_hidden,
    teacher_input,
):
    rep_count = 4
    tokens = student_hidden.shape[0]
    own_rows, model_width = student_weight.shape
    width = rep_count * own_rows
    pair_rows = 2 * own_rows
    me = lax.axis_index("fsdp")
    my_rep = lax.axis_index("rep")
    place = my_rep.astype(jnp.int32).reshape(1)

    def columns(array, flip):
        return lax.dynamic_slice_in_dim(array, (me ^ flip) * width, width, 1)

    cot_x, cot_y = swap_fsdp(out_cotangent, 2), swap_fsdp(out_cotangent, 4)
    share = jnp.sum(
        out_cotangent.astype(jnp.float32) * student_branch.astype(jnp.float32), axis=0
    )
    tail = jnp.stack(three_parts(share)).astype(jnp.bfloat16)
    tail = jnp.pad(tail, ((0, 8 - 3), (0, 0)))
    hidden_of = [jnp.concatenate([columns(student_hidden, 0), columns(student_hidden, 1)], 1)]
    for flip in (2, 4, 6):
        sent = jnp.concatenate([columns(student_hidden, flip), columns(student_hidden, flip + 1)], 1)
        hidden_of.append(swap_fsdp(jnp.concatenate([sent, tail], 0), flip))
    half = tokens // 2
    corner = [swap_fsdp(cot_x[:half], 4), swap_fsdp(cot_y[half:], 2)]
    for hidden in hidden_of[1:]:
        share = share + jnp.sum(hidden[tokens : tokens + 3].astype(jnp.float32), axis=0)

    def scale_it(block):
        scaled = (block.astype(jnp.float32) * layer_scale).astype(jnp.bfloat16)
        return lax.optimization_barrier(scaled)

    keep, send = fold_tokens(layer_scale, hidden_of[:3], [out_cotangent, cot_x, cot_y], width)
    scaled = scale_it(jnp.concatenate(corner, 0))
    far = hidden_of[3][:tokens]
    send = (send + token_fold(far[:, width:], scaled)).astype(jnp.bfloat16)
    keep = keep + token_fold(far[:, :width], scaled)
    share = share + swap_fsdp(share, 1)
    own, *outgoing = split_rows(place, keep, swap_fsdp(send, 1), own_rows, rep_count)
    arrived = [swap_rep(piece, j + 1) for j, piece in enumerate(outgoing)]
    new_weight, new_first, new_second, sent_rows = update_rows(
        place,
        own,
        arrived,
        student_weight,
        first_moment,
        second_moment,
        teacher_weight,
    )

    sent_rows, share = lax.optimization_barrier((sent_rows, share))
    teacher_shard = lax.all_gather(sent_rows, "rep", axis=0, tiled=True)
    share = sum([swap_rep(share, j) for j in range(1, rep_count)], share)
    scale_new, scale_first_new, scale_second_new = adam_step(
        layer_scale, scale_first, scale_second, share
    )
    teacher_scale_new = teacher_keep * teacher_scale + (1.0 - teacher_keep) * scale_new

    along_x, along_y = swap_fsdp(teacher_shard, 2), swap_fsdp(teacher_shard, 4)
    corner_x = swap_fsdp(along_x[:pair_rows], 4)
    corner_y = swap_fsdp(along_y[pair_rows:], 2)

    def terms(block, flip, start):
        total = None
        for weights, f in ((block, flip), (swap_fsdp(block, 1), flip + 1)):
            units = columns(teacher_hidden, f)[:, start : start + block.shape[0]]
            term = jnp.dot(units, weights, preferred_element_type=jnp.float32)
            total = term if total is None else total + term
        return total

    near = teacher_input.astype(jnp.float32) + teacher_scale_new * terms(teacher_shard, 0, 0)
    near = lax.optimization_barrier(near)
    near = near + teacher_scale_new * (terms(along_x, 2, 0) + terms(along_y, 4, 0))
    held_shard = after(teacher_shard, along_x, along_y)
    stored_shard = jnp.where(me >= 0, held_shard, jnp.zeros_like(held_shard))
    swapped_x, swapped_y = swap_fsdp(corner_x, 1), swap_fsdp(corner_y, 1)
    near, stored_shard, swapped_x, swapped_y = lax.optimization_barrier(
        (near, stored_shard, swapped_x, swapped_y)
    )
    far = None
    for block, f, start in (
        (corner_x, 6, 0),
        (corner_y, 6, pair_rows),
        (swapped_x, 7, 0),
        (swapped_y, 7, pair_rows),
    ):
        units = columns(teacher_hidden, f)[:, start : start + pair_rows]
        term = jnp.dot(units, block, preferred_element_type=jnp.float32)
        far = term if far is None else far + term
    teacher_out = (near + teacher_scale_new * far).astype(jnp.bfloat16)
    return (
        new_weight,
        new_first,
        new_second,
        stored_shard,
        scale_new,
        scale_first_new,
        scale_second_new,
        teacher_scale_new,
        teacher_out,
    )


def shards(*args):
    hidden, weight = args[0], args[6]
    rows, model_width = weight.shape
    fits = (
        lax.axis_size("fsdp") == 8
        and lax.axis_size("rep") == 4
        and rows % 32 == 0
        and hidden.shape[0] % 32 == 0
        and 8 * rows == model_width
        and model_width % 256 == 0
    )
    return block_shards(*args) if fits else general_shards(*args)


def solution(mesh):
    in_specs = (
        P(("fsdp", "rep"), None),
        P(("fsdp", "rep"), None),
        P(("fsdp", "rep"), None),
        P(),
        P(),
        P(),
        P(("fsdp", "rep"), None),
        P(("fsdp", "rep"), None),
        P(("fsdp", "rep"), None),
        P("fsdp", None),
        P(),
        P(("fsdp", "rep"), None),
        P(("fsdp", "rep"), None),
    )
    out_specs = (
        P(("fsdp", "rep"), None),
        P(("fsdp", "rep"), None),
        P(("fsdp", "rep"), None),
        P("fsdp", None),
        P(),
        P(),
        P(),
        P(),
        P(("fsdp", "rep"), None),
    )
    return jax.shard_map(shards, mesh=mesh, in_specs=in_specs, out_specs=out_specs, check_vma=False)
```

```python
import jax
import jax.numpy as jnp
from jax import lax
from jax.experimental import pallas as pl
from jax.experimental.pallas import tpu as pltpu
from jax.sharding import PartitionSpec as P

beta_one = 0.9
beta_two = 0.95
learn_rate = 0.02
epsilon = 1e-08
teacher_keep = 0.75

BOTH = ("fsdp", "rep")


def adam_step(values, moment_one, moment_two, gradient):
    first_new = beta_one * moment_one.astype(jnp.float32) + (1.0 - beta_one) * gradient
    second_new = beta_two * moment_two.astype(jnp.float32) + (1.0 - beta_two) * gradient * gradient
    values_new = values.astype(jnp.float32) - learn_rate * first_new / (
        jnp.sqrt(second_new) + epsilon
    )
    return (values_new, first_new, second_new)


def token_fold(arrived, portion):
    return lax.dot_general(
        arrived, portion, (((0,), (0,)), ((), ())), preferred_element_type=jnp.float32
    )


def swap_fsdp(value, flip):
    count = lax.axis_size("fsdp")
    return lax.ppermute(value, "fsdp", [(i, i ^ flip) for i in range(count)])


def swap_rep(value, flip):
    count = lax.axis_size("rep")
    return lax.ppermute(value, "rep", [(i, i ^ flip) for i in range(count)])


def gather_chips(value, chips):
    rows = value.shape[0]
    if chips == 4 and rows % 32 == 0:
        along_x = swap_fsdp(value, 2)
        along_y = swap_fsdp(value, 4)
        half = rows // 2
        corner = [swap_fsdp(along_x[:half], 4), swap_fsdp(along_y[half:], 2)]
        return [[value], [along_x], [along_y], corner]
    return [[value]] + [[swap_fsdp(value, 2 * j)] for j in range(1, chips)]


def all_sum(value):
    flip = 1
    while flip < lax.axis_size("rep"):
        value = value + swap_rep(value, flip)
        flip *= 2
    flip = 1
    while flip < lax.axis_size("fsdp"):
        value = value + swap_fsdp(value, flip)
        flip *= 2
    return value


def general_shards(
    student_hidden,
    out_cotangent,
    student_branch,
    layer_scale,
    scale_first,
    scale_second,
    student_weight,
    first_moment,
    second_moment,
    teacher_weight,
    teacher_scale,
    teacher_hidden,
    teacher_input,
):
    fsdp_count = lax.axis_size("fsdp")
    rep_count = lax.axis_size("rep")
    chips = fsdp_count // 2
    own_rows = student_weight.shape[0]
    width = rep_count * own_rows
    me = lax.axis_index("fsdp")
    my_rep = lax.axis_index("rep")

    def columns(array, flip):
        return lax.dynamic_slice_in_dim(array, (me ^ flip) * width, width, 1)

    cotangent = out_cotangent.astype(jnp.float32)
    scale_grad = all_sum(jnp.sum(cotangent * student_branch.astype(jnp.float32), axis=0))
    scale_new, scale_first_new, scale_second_new = adam_step(
        layer_scale, scale_first, scale_second, scale_grad
    )
    teacher_scale_new = teacher_keep * teacher_scale + (1.0 - teacher_keep) * scale_new

    scaled = (cotangent * layer_scale).astype(jnp.bfloat16)
    scaled_of = [jnp.concatenate(b, 0) if len(b) > 1 else b[0] for b in gather_chips(scaled, chips)]
    partial_term = None
    for j in range(chips):
        sent = jnp.concatenate([columns(student_hidden, 2 * j), columns(student_hidden, 2 * j + 1)], 1)
        arrived = swap_fsdp(sent, 2 * j) if j else sent
        term = token_fold(arrived, scaled_of[j])
        partial_term = term if partial_term is None else partial_term + term
    pair = partial_term[:width] + swap_fsdp(partial_term[width:], 1)

    def rows_of(array, flip):
        return lax.dynamic_slice_in_dim(array, (my_rep ^ flip) * own_rows, own_rows, 0)

    gradient = rows_of(pair, 0)
    for j in range(1, rep_count):
        gradient = gradient + swap_rep(rows_of(pair, j).astype(jnp.bfloat16), j).astype(jnp.float32)
    weight_new, first_new, second_new = adam_step(
        student_weight, first_moment, second_moment, gradient
    )
    teacher_rows = (
        teacher_keep * rows_of(teacher_weight, 0).astype(jnp.float32)
        + (1.0 - teacher_keep) * weight_new
    ).astype(jnp.bfloat16)
    teacher_shard = jnp.zeros((width,) + teacher_rows.shape[1:], jnp.bfloat16)
    for j in range(rep_count):
        piece = swap_rep(teacher_rows, j) if j else teacher_rows
        teacher_shard = lax.dynamic_update_slice_in_dim(
            teacher_shard, piece, (my_rep ^ j) * own_rows, 0
        )
    projected = None
    for j, blocks in enumerate(gather_chips(teacher_shard, chips)):
        low, high = columns(teacher_hidden, 2 * j), columns(teacher_hidden, 2 * j + 1)
        start = 0
        for block in blocks:
            stop = start + block.shape[0]
            for hidden, weights in ((low, block), (high, swap_fsdp(block, 1))):
                term = jnp.dot(hidden[:, start:stop], weights, preferred_element_type=jnp.float32)
                projected = term if projected is None else projected + term
            start = stop
    teacher_out = (teacher_input.astype(jnp.float32) + teacher_scale_new * projected).astype(
        jnp.bfloat16
    )
    return (
        weight_new.astype(jnp.bfloat16),
        first_new.astype(jnp.bfloat16),
        second_new.astype(jnp.bfloat16),
        teacher_shard,
        scale_new,
        scale_first_new,
        scale_second_new,
        teacher_scale_new,
        teacher_out,
    )


def after(value, *others):
    return lax.optimization_barrier((value,) + others)[0]


MIB = 1024 * 1024
VMEM = pl.BlockSpec(memory_space=pltpu.VMEM)
SMEM = pl.BlockSpec(memory_space=pltpu.SMEM)


def three_parts(value):
    high = lax.reduce_precision(value, 8, 7)
    rest = value - high
    mid = lax.reduce_precision(rest, 8, 7)
    return [high, mid, rest - mid]


def fold_kernel(scale, *refs):
    hidden, cotangent, (keep, send) = refs[:3], refs[3:6], refs[6:]
    width = keep.shape[0]
    tokens = cotangent[0].shape[0]
    parts = [None, None]
    for h, c in zip(hidden, cotangent):
        scaled = (c[...].astype(jnp.float32) * scale[...]).astype(jnp.bfloat16)
        for k in range(2):
            term = token_fold(h[:tokens, k * width : (k + 1) * width], scaled)
            parts[k] = term if parts[k] is None else parts[k] + term
    keep[...] = parts[0]
    send[...] = parts[1]


def fold_tokens(scale, hidden, cotangent, width):
    model_width = cotangent[0].shape[1]
    total = jax.ShapeDtypeStruct((width, model_width), jnp.float32)
    return pl.pallas_call(
        fold_kernel,
        out_shape=[total, total],
        in_specs=[VMEM] * 7,
        out_specs=[VMEM] * 2,
        compiler_params=pltpu.CompilerParams(vmem_limit_bytes=24 * MIB),
        cost_estimate=pl.CostEstimate(
            flops=12 * cotangent[0].size * width,
            bytes_accessed=4 * model_width * width + 12 * cotangent[0].size,
            transcendentals=0,
        ),
        name="fold_tokens",
    )(scale.reshape(1, -1), *hidden, *cotangent)


def finish_kernel(scale, hidden, upper, lower, before, out, held):
    width, half = out.shape[0], upper.shape[0]
    for i, block in enumerate((upper, lower)):
        held[i * half : (i + 1) * half, :] = (
            block[...].astype(jnp.float32) * scale[...]
        ).astype(jnp.bfloat16)
    tokens = 2 * half
    total = before[...] + token_fold(hidden[:tokens, width:], held[...])
    out[...] = total.astype(jnp.bfloat16)


def finish_send(scale, hidden, corner, before):
    width, model_width = before.shape
    tokens = 2 * corner[0].shape[0]
    return pl.pallas_call(
        finish_kernel,
        out_shape=[
            jax.ShapeDtypeStruct((width, model_width), jnp.bfloat16),
            jax.ShapeDtypeStruct((tokens, model_width), jnp.bfloat16),
        ],
        in_specs=[VMEM] * 5,
        out_specs=[VMEM] * 2,
        compiler_params=pltpu.CompilerParams(vmem_limit_bytes=24 * MIB),
        cost_estimate=pl.CostEstimate(
            flops=2 * tokens * width * model_width,
            bytes_accessed=6 * width * model_width + 8 * tokens * model_width,
            transcendentals=0,
        ),
        name="finish_send",
    )(scale.reshape(1, -1), hidden, *corner, before)


def split_kernel(place, keep, arrived, own, *outgoing):
    rows = own.shape[0]
    for j in range(len(outgoing) + 1):
        at = pl.ds(pl.multiple_of((place[0] ^ j) * rows, 32), rows)
        total = keep[at, :] + arrived[at, :].astype(jnp.float32)
        if j:
            outgoing[j - 1][...] = total.astype(jnp.bfloat16)
        else:
            own[...] = total


def split_rows(place, keep, arrived, rows, count):
    width = keep.shape[1]
    return pl.pallas_call(
        split_kernel,
        out_shape=[jax.ShapeDtypeStruct((rows, width), jnp.float32)]
        + [jax.ShapeDtypeStruct((rows, width), jnp.bfloat16)] * (count - 1),
        in_specs=[SMEM, VMEM, VMEM],
        out_specs=[VMEM] * count,
        compiler_params=pltpu.CompilerParams(vmem_limit_bytes=24 * MIB),
        cost_estimate=pl.CostEstimate(
            flops=keep.size, bytes_accessed=11 * keep.size, transcendentals=0
        ),
        name="split_rows",
    )(place, keep, arrived)


def update_kernel(own, one, two, three, weight, first, second, teacher, *outs):
    new_weight, new_first, new_second, sent = outs
    gradient = own[...] + one[...].astype(jnp.float32)
    gradient = gradient + two[...].astype(jnp.float32) + three[...].astype(jnp.float32)
    weight_new, first_new, second_new = adam_step(
        weight[...], first[...], second[...], gradient
    )
    new_weight[...] = weight_new.astype(jnp.bfloat16)
    new_first[...] = first_new.astype(jnp.bfloat16)
    new_second[...] = second_new.astype(jnp.bfloat16)
    held = teacher[...].astype(jnp.float32)
    sent[...] = (teacher_keep * held + (1.0 - teacher_keep) * weight_new).astype(jnp.bfloat16)


def update_rows(own, arrived, weight, first, second, teacher):
    rows, width = own.shape
    stored = jax.ShapeDtypeStruct((rows, width), jnp.bfloat16)
    return pl.pallas_call(
        update_kernel,
        out_shape=[stored] * 4,
        in_specs=[VMEM] * 8,
        out_specs=[VMEM] * 4,
        compiler_params=pltpu.CompilerParams(vmem_limit_bytes=24 * MIB),
        cost_estimate=pl.CostEstimate(
            flops=20 * own.size, bytes_accessed=30 * own.size, transcendentals=2 * own.size
        ),
        name="update_rows",
    )(own, *arrived, weight, first, second, teacher)


def block_shards(
    student_hidden,
    out_cotangent,
    student_branch,
    layer_scale,
    scale_first,
    scale_second,
    student_weight,
    first_moment,
    second_moment,
    teacher_weight,
    teacher_scale,
    teacher_hidden,
    teacher_input,
):
    rep_count = 4
    tokens = student_hidden.shape[0]
    own_rows, model_width = student_weight.shape
    width = rep_count * own_rows
    pair_rows = 2 * own_rows
    me = lax.axis_index("fsdp")
    my_rep = lax.axis_index("rep")
    place = my_rep.astype(jnp.int32).reshape(1)

    def columns(array, flip):
        return lax.dynamic_slice_in_dim(array, (me ^ flip) * width, width, 1)

    cot_x, cot_y = swap_fsdp(out_cotangent, 2), swap_fsdp(out_cotangent, 4)
    share = jnp.sum(
        out_cotangent.astype(jnp.float32) * student_branch.astype(jnp.float32), axis=0
    )
    tail = jnp.stack(three_parts(share)).astype(jnp.bfloat16)
    tail = jnp.pad(tail, ((0, 8 - 3), (0, 0)))
    hidden_of = [jnp.concatenate([columns(student_hidden, 0), columns(student_hidden, 1)], 1)]
    for flip in (2, 4, 6):
        sent = jnp.concatenate([columns(student_hidden, flip), columns(student_hidden, flip + 1)], 1)
        hidden_of.append(swap_fsdp(jnp.concatenate([sent, tail], 0), flip))
    half = tokens // 2
    corner = [swap_fsdp(cot_x[:half], 4), swap_fsdp(cot_y[half:], 2)]
    for hidden in hidden_of[1:]:
        share = share + jnp.sum(hidden[tokens : tokens + 3].astype(jnp.float32), axis=0)

    keep, send = fold_tokens(layer_scale, hidden_of[:3], [out_cotangent, cot_x, cot_y], width)
    send, scaled = finish_send(layer_scale, hidden_of[3], corner, send)
    far = hidden_of[3][:tokens]
    keep = keep + token_fold(far[:, :width], scaled)
    share = share + swap_fsdp(share, 1)
    own, *outgoing = split_rows(place, keep, swap_fsdp(send, 1), own_rows, rep_count)
    arrived = [swap_rep(piece, j + 1) for j, piece in enumerate(outgoing)]
    new_weight, new_first, new_second, sent_rows = update_rows(
        own,
        arrived,
        student_weight,
        first_moment,
        second_moment,
        lax.dynamic_slice_in_dim(teacher_weight, my_rep * own_rows, own_rows, 0),
    )

    sent_rows, share = lax.optimization_barrier((sent_rows, share))
    teacher_shard = lax.all_gather(sent_rows, "rep", axis=0, tiled=True)
    share = sum([swap_rep(share, j) for j in range(1, rep_count)], share)
    scale_new, scale_first_new, scale_second_new = adam_step(
        layer_scale, scale_first, scale_second, share
    )
    teacher_scale_new = teacher_keep * teacher_scale + (1.0 - teacher_keep) * scale_new

    along_x, along_y = swap_fsdp(teacher_shard, 2), swap_fsdp(teacher_shard, 4)
    corner_x = swap_fsdp(along_x[:pair_rows], 4)
    corner_y = swap_fsdp(along_y[pair_rows:], 2)

    def terms(block, flip, start):
        total = None
        for weights, f in ((block, flip), (swap_fsdp(block, 1), flip + 1)):
            units = columns(teacher_hidden, f)[:, start : start + block.shape[0]]
            term = jnp.dot(units, weights, preferred_element_type=jnp.float32)
            total = term if total is None else total + term
        return total

    near = teacher_input.astype(jnp.float32) + teacher_scale_new * terms(teacher_shard, 0, 0)
    near = lax.optimization_barrier(near)
    near = near + teacher_scale_new * (terms(along_x, 2, 0) + terms(along_y, 4, 0))
    held_shard = after(teacher_shard, along_x, along_y)
    stored_shard = jnp.where(me >= 0, held_shard, jnp.zeros_like(held_shard))
    swapped_x, swapped_y = swap_fsdp(corner_x, 1), swap_fsdp(corner_y, 1)
    near, stored_shard, swapped_x, swapped_y = lax.optimization_barrier(
        (near, stored_shard, swapped_x, swapped_y)
    )
    far = None
    for block, f, start in (
        (corner_x, 6, 0),
        (corner_y, 6, pair_rows),
        (swapped_x, 7, 0),
        (swapped_y, 7, pair_rows),
    ):
        units = columns(teacher_hidden, f)[:, start : start + pair_rows]
        term = jnp.dot(units, block, preferred_element_type=jnp.float32)
        far = term if far is None else far + term
    teacher_out = (near + teacher_scale_new * far).astype(jnp.bfloat16)
    return (
        new_weight,
        new_first,
        new_second,
        stored_shard,
        scale_new,
        scale_first_new,
        scale_second_new,
        teacher_scale_new,
        teacher_out,
    )


def shards(*args):
    hidden, weight = args[0], args[6]
    rows, model_width = weight.shape
    fits = (
        lax.axis_size("fsdp") == 8
        and lax.axis_size("rep") == 4
        and rows % 32 == 0
        and hidden.shape[0] % 32 == 0
        and 8 * rows == model_width
        and model_width % 256 == 0
    )
    return block_shards(*args) if fits else general_shards(*args)


def solution(mesh):
    in_specs = (
        P(("fsdp", "rep"), None),
        P(("fsdp", "rep"), None),
        P(("fsdp", "rep"), None),
        P(),
        P(),
        P(),
        P(("fsdp", "rep"), None),
        P(("fsdp", "rep"), None),
        P(("fsdp", "rep"), None),
        P("fsdp", None),
        P(),
        P(("fsdp", "rep"), None),
        P(("fsdp", "rep"), None),
    )
    out_specs = (
        P(("fsdp", "rep"), None),
        P(("fsdp", "rep"), None),
        P(("fsdp", "rep"), None),
        P("fsdp", None),
        P(),
        P(),
        P(),
        P(),
        P(("fsdp", "rep"), None),
    )
    return jax.shard_map(shards, mesh=mesh, in_specs=in_specs, out_specs=out_specs, check_vma=False)
```
